32 devices in a mesh: wave: 8 (over z, x), parity: 2 (over y), lev: 2 (over core).
Axes of the slice: x: 2, y: 2, z: 4, core: 2. Of those that a mesh axis runs over, the one named last changes fastest.
Arguments:
- fourier: bfloat16 [2, 1280, 16, 256], P('parity', 'wave', None, 'lev'), may hold values from -6 to 6
- legendre: bfloat16 [16, 2, 1280, 1280], P('wave', 'parity', 'lev'), may hold values from -0.15625 to 0.15625
- quad_weights: float32 [1280], P('wave'), may hold values from 0.3 to 3
- slot_wave: int32 [16], replicated, may hold values from 0 to 15, as said below
- to_modes: float32 [128, 128], replicated, may hold values from -0.5 to 0.5
- from_modes: float32 [128, 128], replicated, may hold values from -0.5 to 0.5
- mode_rates: float32 [128], replicated, may hold values from 0.1 to 10
Outputs:
- columns: bfloat16 [2, 1280, 16, 256], P('parity', 'wave', None, 'lev')
- spectral: bfloat16 [2, 1280, 4096], P('parity', 'lev', 'wave')
The draws below stay inside these ranges and needn't reach their ends.
Inputs may be any that keep to these rules, and one draw needn't show every extreme that they name: `slot_wave`: A permutation of the wavenumbers 0 to 15; the owner with index w on wave holds slots w * 2 to (w + 1) * 2 - 1. Slots 2 i and 2 i + 1 hold a wavenumber below 8 and 15 minus it, in that order.
All inputs are finite; a program needn't handle non-finite values.
Results may differ from the reference program's by a relative error of at most 0.014.
Values may be sent and summed in bfloat16 or wider, within the bound.
No kernel may reach another device: no remote copies, remote signals or barrier semaphores. Data moves between devices by JAX's collectives and lax.ppermute only.
A program may use at most 128 MiB of HBM per device.

```python
import math
import jax
import jax.numpy as jnp
from jax import lax

NLAT_H = 1280
NDEG_H = 1280
LEVELS = 128
M_DEV = 2
WAVES = 16


def draw_slot_wave(key, part):
    if M_DEV % 2 == 0:
        low_half = jax.random.permutation(key, WAVES // 2).astype(jnp.int32)
        return jnp.stack([low_half, WAVES - 1 - low_half], axis=1).reshape(-1).astype(jnp.int32)
    return jax.random.permutation(key, WAVES).astype(jnp.int32)


def shard_levels(key, extent, cuts, low, top_value):
    def one(dim, blocks):
        heights = jax.random.uniform(jax.random.fold_in(jax.random.fold_in(key, 6), dim), (blocks,), jnp.float32, low / len(cuts), top_value / len(cuts))
        return jnp.repeat(jnp.exp(heights), extent[dim] // blocks).reshape((-1,) + (1,) * (len(extent) - dim - 1))

    level = one(*cuts[0])
    for cut in cuts[1:]:
        level = level * one(*cut)
    return level


def bell_draw(rng, dims, spread, reach, pieces=(), held_as=jnp.bfloat16):
    result = spread * jax.random.normal(rng, dims, jnp.float32)
    if pieces:
        result = result * shard_levels(rng, dims, pieces, -0.22, 0.18)
    return jnp.clip(result, -reach, reach).astype(held_as)


def setup_inputs(seed: int = 0) -> dict:
    key_list = jax.random.split(jax.random.key(seed), 8)
    return {
        "fourier": bell_draw(key_list[0], (2, NLAT_H, WAVES, 2 * LEVELS), 1.0, 6.0, ((0, 2), (1, 8), (3, 2))),
        "legendre": bell_draw(key_list[1], (WAVES, 2, NLAT_H, NDEG_H), NLAT_H ** -0.5, 0.15625, ((0, 8), (1, 2), (2, 2))),
        "quad_weights": jnp.clip(jnp.exp(math.log(3.0) - 2.3025851 * jax.random.uniform(key_list[2], (NLAT_H,), jnp.float32) ** shard_levels(key_list[2], (NLAT_H,), ((0, 8),), -0.2, 0.2)), 0.3, 3.0),
        "slot_wave": draw_slot_wave(jax.random.fold_in(key_list[7], 71), 0),
        "to_modes": bell_draw(key_list[4], (LEVELS, LEVELS), LEVELS ** -0.5, 0.5, (), jnp.float32),
        "from_modes": bell_draw(key_list[5], (LEVELS, LEVELS), LEVELS ** -0.5, 0.5, (), jnp.float32),
        "mode_rates": jnp.clip(jnp.exp(jax.random.uniform(key_list[6], (LEVELS,), jnp.float32, math.log(0.1), math.log(10.0))), 0.1, 10.0),
    }


def reference(fourier, legendre, quad_weights, slot_wave, to_modes, from_modes, mode_rates):
    top_degree = 2 * NDEG_H - 1
    scaled = (quad_weights[None, :, None, None] * fourier.astype(jnp.float32)).astype(jnp.bfloat16)
    widened = scaled.astype(jnp.float32)
    folded = jnp.stack([widened[0] + widened[1], widened[0] - widened[1]]).astype(jnp.bfloat16)
    by_slot = jnp.moveaxis(jnp.take(folded, slot_wave, axis=2), 2, 0)
    parity_idx = jnp.arange(2, dtype=jnp.int32)
    degree_idx = jnp.arange(NDEG_H, dtype=jnp.int32)

    def per_slot(operands):
        rows_table, rows_data, wavenum = operands
        table_wide = rows_table.astype(jnp.float32)
        raw = jnp.einsum("qjk,qjc->qkc", table_wide, rows_data.astype(jnp.float32))
        degree = (wavenum + 2 * degree_idx[None, :] + parity_idx[:, None]).astype(jnp.int32)
        kept = jnp.where((degree <= top_degree)[:, :, None], raw, jnp.zeros_like(raw))
        shaped = kept.reshape(2, NDEG_H, LEVELS, 2)
        mode_part = jnp.einsum("il,qklr->qkir", to_modes, shaped, precision=lax.Precision.HIGHEST)
        degree_f = degree.astype(jnp.float32)
        stiffness = degree_f * (degree_f + 1.0) / (top_degree * (top_degree + 1.0))
        mode_part = mode_part / (1.0 + stiffness[:, :, None, None] * mode_rates[None, None, :, None])
        updated = jnp.einsum("li,qkir->qklr", from_modes, mode_part, precision=lax.Precision.HIGHEST)
        updated = updated.reshape(2, NDEG_H, 2 * LEVELS).astype(jnp.bfloat16)
        parts = jnp.einsum("qjk,qkc->qjc", table_wide, updated.astype(jnp.float32)).astype(jnp.bfloat16)
        return updated, parts

    updated_all, parts_all = lax.map(per_slot, (legendre, by_slot, slot_wave))
    wave_count = slot_wave.shape[0]
    spectral = jnp.transpose(updated_all, (1, 2, 0, 3)).reshape(2, NDEG_H, wave_count * 2 * LEVELS)
    wide_parts = parts_all.astype(jnp.float32)
    joined = jnp.stack([wide_parts[:, 0] + wide_parts[:, 1], wide_parts[:, 0] - wide_parts[:, 1]]).astype(jnp.bfloat16)
    inverse_slot = jnp.zeros((wave_count,), jnp.int32).at[slot_wave].set(jnp.arange(wave_count, dtype=jnp.int32))
    columns = jnp.transpose(jnp.take(joined, inverse_slot, axis=1), (0, 2, 1, 3))
    return columns, spectral
```

```python
import functools

import jax
import jax.numpy as jnp
from jax import lax
from jax.experimental import pallas as pl
from jax.experimental.pallas import tpu as pltpu
from jax.sharding import PartitionSpec as P

AXES = ("wave", "parity", "lev")
VMEM = pl.BlockSpec(memory_space=pltpu.VMEM)
SMEM = pl.BlockSpec(memory_space=pltpu.SMEM)
MIB = 1024 * 1024


def partner_2(value, axis, distance):
    mask = 2**distance
    pairs = [(source, source ^ mask) for source in range(lax.axis_size(axis))]
    return lax.ppermute(value, axis, pairs)


def combine(mine_part, partner, signed_one):
    return (partner.astype(jnp.float32) + signed_one * mine_part.astype(jnp.float32)).astype(
        jnp.bfloat16
    )


def mask_plan(owners):
    ring = owners // 2

    def hops(mask):
        step = mask >> 1
        return min(step, ring - step) + (mask & 1)

    plan = []
    for core in range(2):
        masks = [m for m in range(owners) if (m >> 1) & 1 == core]
        masks.sort(key=lambda m: (hops(m), m))
        half = len(masks) // 2
        plan.append((masks[:half], masks[half:]))
    return plan


def meet(value, masks):
    owners, hemis = lax.axis_size("wave"), lax.axis_size("parity")
    pairs = []
    for wave in range(owners):
        for hemi in range(hemis):
            for core, mask in enumerate(masks):
                if mask:
                    source = (wave * hemis + hemi) * 2 + core
                    target = ((wave ^ mask) * hemis + hemi) * 2 + core
                    pairs.append((source, target))
    return lax.ppermute(value, AXES, pairs)


def near_exchange(blocks, plan, lev):
    arrived = []
    for i, block in enumerate(blocks):
        masks = (plan[0][0][i], plan[1][0][i])
        got = meet(block, masks)
        if not masks[0]:
            got = jnp.where(lev == 0, block, got)
        arrived.append(got)
    keep = jnp.stack([a[0] for a in arrived])
    give = jnp.stack([a[1] for a in arrived])
    got = partner_2(give, "lev", 0)
    return keep, partner_2(keep, "parity", 0), got, partner_2(got, "parity", 0)


def far_exchange(blocks, plan):
    arrived = [
        meet(block, (plan[0][1][i], plan[1][1][i])) for i, block in enumerate(blocks)
    ]
    give = jnp.stack([a[1] for a in arrived])
    return arrived, partner_2(give, "lev", 0)


def scale_kernel(meta, slots, mine, other, weights, near, far, held):
    rows, waves, width = mine.shape
    lev = meta[0]
    held[0] = mine[...].astype(jnp.float32).reshape(rows * waves, width)
    held[1] = other[...].astype(jnp.float32).reshape(rows * waves, width)
    scale = weights[...]
    count = near.shape[0]
    for out, base in ((near, 1), (far, 1 + count)):
        for i in range(count):
            owner = meta[base + i]
            for part in range(2):
                slot = 2 * owner + (lev if part == 0 else 1 - lev)
                wave = slots[slot]
                for source in range(2):
                    picked = held[source, pl.ds(wave, rows, stride=waves), :]
                    place = (lev if source == 0 else 1 - lev) * width
                    out[i, part, :, pl.ds(pl.multiple_of(place, width), width)] = (
                        scale * picked
                    ).astype(jnp.bfloat16)


def solve_kernel(
    meta,
    keep,
    keep_peer,
    got,
    got_peer,
    *refs,
    count,
):
    far = refs[:count]
    far_got, table_mine, table_other, to_modes, from_modes, rates = refs[count : count + 6]
    (spec_mine, spec_other, near_mine, near_other, far_mine, far_other, data, spec, parts) = refs[
        count + 6 :
    ]
    lev, parity, wavenum = meta[0], meta[1], meta[2]
    rows = keep.shape[1]
    half, degrees = table_mine.shape
    width = data.shape[1]
    sign = (1 - 2 * parity).astype(jnp.float32)

    def place(index):
        return pl.ds(pl.multiple_of(meta[3 + index] * rows, 16), rows)

    def fold(own, peer):
        return (peer.astype(jnp.float32) + sign * own.astype(jnp.float32)).astype(jnp.bfloat16)

    for i in range(count):
        data[place(i), :] = fold(keep[i], keep_peer[i])
        data[place(count + i), :] = fold(got[i], got_peer[i])
        data[place(2 * count + i), :] = far[i][0]
        data[place(3 * count + i), :] = far_got[i]
    at_mine = pl.ds(pl.multiple_of(lev * half, 16), half)
    at_other = pl.ds(pl.multiple_of((1 - lev) * half, 16), half)
    rows_first = (((0,), (0,)), ((), ()))
    raw = lax.dot_general(
        data[at_mine, :], table_mine[...], rows_first, preferred_element_type=jnp.float32
    ) + lax.dot_general(
        data[at_other, :], table_other[...], rows_first, preferred_element_type=jnp.float32
    )
    top_degree = 2 * degrees - 1
    degree = wavenum + parity + 2 * lax.broadcasted_iota(jnp.int32, (1, degrees), 1)
    kept = jnp.where(degree <= top_degree, raw, 0.0)
    degree_f = degree.astype(jnp.float32)
    stiffness = degree_f * (degree_f + 1.0) / (top_degree * (top_degree + 1.0))

    levels = to_modes.shape[0]
    spread = (
        (lax.broadcasted_iota(jnp.int32, (width, levels), 0) >> 1)
        == lax.broadcasted_iota(jnp.int32, (width, levels), 1)
    ).astype(jnp.float32)
    same = (
        (
            lax.broadcasted_iota(jnp.int32, (width, width), 0)
            + lax.broadcasted_iota(jnp.int32, (width, width), 1)
        )
        & 1
    ) == 0
    exact = functools.partial(
        lax.dot_general,
        precision=lax.Precision.HIGHEST,
        preferred_element_type=jnp.float32,
    )
    plain = (((1,), (0,)), ((), ()))

    def widen(square):
        tall = exact(spread, square[...], plain)
        return jnp.where(same, exact(tall, spread, (((1,), (1,)), ((), ()))), 0.0)

    rate = jnp.sum(spread * rates[...], axis=1, keepdims=True)
    modal = exact(widen(to_modes), kept, plain)
    damped = modal / (1.0 + stiffness * rate)
    updated = exact(widen(from_modes), damped, plain)
    spec[...] = jnp.transpose(updated).astype(jnp.bfloat16)
    part_mine = jnp.dot(table_mine[...], spec[...], preferred_element_type=jnp.float32)
    parts[at_mine, :] = part_mine.astype(jnp.bfloat16)
    part_other = jnp.dot(table_other[...], spec[...], preferred_element_type=jnp.float32)
    parts[at_other, :] = part_other.astype(jnp.bfloat16)
    spec_mine[...] = spec[at_mine, :]
    spec_other[...] = spec[at_other, :]
    side = width // 2
    first = pl.ds(pl.multiple_of(lev * side, side), side)
    second = pl.ds(pl.multiple_of((1 - lev) * side, side), side)
    for out, base, order in (
        (near_mine, 0, (first, second)),
        (near_other, count, (second, first)),
        (far_mine, 2 * count, (first, second)),
        (far_other, 3 * count, (second, first)),
    ):
        for i in range(count):
            for part in range(2):
                out[i, part] = parts[place(base + i), order[part]]


def place_kernel(meta, slots, keep, keep_peer, got, got_peer, *refs, count):
    far = refs[:count]
    far_got, out, held = refs[count:]
    lev, parity = meta[0], meta[1]
    rows, waves, width = out.shape
    sign = (1 - 2 * parity).astype(jnp.float32)

    def fold(own, peer):
        return (peer.astype(jnp.float32) + sign * own.astype(jnp.float32)).astype(jnp.bfloat16)

    for i in range(count):
        for part in range(2):
            mine = lev if part == 0 else 1 - lev
            other = 1 - mine
            for index, core, value in (
                (i, mine, fold(keep[i, part], keep_peer[i, part])),
                (count + i, other, fold(got[i, part], got_peer[i, part])),
                (2 * count + i, mine, far[i][0, part]),
                (3 * count + i, other, far_got[i, part]),
            ):
                wave = slots[2 * meta[3 + index] + core]
                held[pl.ds(wave, rows, stride=waves), :] = value.astype(jnp.float32)
    out[...] = held[...].reshape(rows, waves, width).astype(jnp.bfloat16)


def params(mebibytes):
    return pltpu.CompilerParams(vmem_limit_bytes=mebibytes * MIB)


def per_device(fourier, legendre, quad_weights, slot_wave, to_modes, from_modes, mode_rates):
    wave = lax.axis_index("wave").astype(jnp.int32)
    parity = lax.axis_index("parity").astype(jnp.int32)
    lev = lax.axis_index("lev").astype(jnp.int32)
    signed_one = (1 - 2 * parity).astype(jnp.float32)
    owners = lax.axis_size("wave")
    plan = mask_plan(owners)
    count = owners // 4
    rows, waves, side = fourier.shape[1:]
    width = 2 * side
    half, degrees = legendre.shape[2:]
    bf16 = jnp.bfloat16

    def masks(core, kind):
        return jnp.asarray(plan[core][kind], jnp.int32)

    def owners_met(kind, sibling):
        first, second = masks(0, kind), masks(1, kind)
        return wave ^ jnp.where((lev == 0) != sibling, first, second)

    near_ids, near_ids_other = owners_met(0, False), owners_met(0, True)
    far_ids, far_ids_other = owners_met(1, False), owners_met(1, True)

    grid_mine = fourier[0]
    grid_other = partner_2(grid_mine, "lev", 0)
    block = jax.ShapeDtypeStruct((count, 2, rows, width), bf16)
    near, far = pl.pallas_call(
        scale_kernel,
        out_shape=(block, block),
        in_specs=[SMEM, SMEM, VMEM, VMEM, VMEM],
        out_specs=(VMEM, VMEM),
        scratch_shapes=[pltpu.VMEM((2, rows * waves, side), jnp.float32)],
        compiler_params=params(16),
        name="scale",
    )(
        jnp.concatenate([lev[None], near_ids, far_ids]),
        slot_wave,
        grid_mine,
        grid_other,
        quad_weights[:, None],
    )
    far_folded = combine(far, partner_2(far, "parity", 0), signed_one)
    near_parts = near_exchange([near[i] for i in range(count)], plan, lev)
    far_arrived, far_got = far_exchange([far_folded[i] for i in range(count)], plan)

    table_mine = lax.dynamic_index_in_dim(legendre[:, 0], lev, 0, False)
    table_other = partner_2(lax.dynamic_index_in_dim(legendre[:, 0], 1 - lev, 0, False), "lev", 0)
    wavenum = lax.dynamic_slice_in_dim(slot_wave, 2 * wave + lev, 1)
    meta = jnp.concatenate(
        [lev[None], parity[None], wavenum, near_ids, near_ids_other, far_ids, far_ids_other]
    )
    spec_shape = jax.ShapeDtypeStruct((half, width), bf16)
    piece = jax.ShapeDtypeStruct((count, 2, rows, side), bf16)
    outs = pl.pallas_call(
        functools.partial(solve_kernel, count=count),
        out_shape=(spec_shape, spec_shape, piece, piece, piece, piece),
        in_specs=[SMEM] + [VMEM] * (10 + count),
        out_specs=(VMEM,) * 6,
        scratch_shapes=[pltpu.VMEM((2 * half, width), bf16)] * 3,
        compiler_params=params(32),
        name="solve",
    )(
        meta,
        *near_parts,
        *far_arrived,
        far_got,
        table_mine,
        table_other,
        to_modes,
        from_modes,
        mode_rates[None, :],
    )
    spec_mine, spec_other, near_mine, near_other, far_mine, far_other = outs
    spec_got = partner_2(spec_other, "lev", 0)
    spectral = jnp.where(
        lev == 0,
        jnp.concatenate([spec_mine, spec_got], axis=1),
        jnp.concatenate([spec_got, spec_mine], axis=1),
    )

    far_from_other = partner_2(far_other, "lev", 0)
    near_from_other = partner_2(near_other, "lev", 0)
    far_folded = jnp.stack(
        [
            combine(far_mine, partner_2(far_mine, "parity", 0), signed_one),
            combine(far_from_other, partner_2(far_from_other, "parity", 0), signed_one),
        ],
        axis=2,
    )
    near = jnp.stack([near_mine, near_from_other], axis=2)
    near_parts = near_exchange([near[i] for i in range(count)], plan, lev)
    far_arrived, far_got = far_exchange([far_folded[i] for i in range(count)], plan)
    columns = pl.pallas_call(
        functools.partial(place_kernel, count=count),
        out_shape=jax.ShapeDtypeStruct((rows, waves, side), bf16),
        in_specs=[SMEM, SMEM] + [VMEM] * (5 + count),
        out_specs=VMEM,
        scratch_shapes=[pltpu.VMEM((rows * waves, side), jnp.float32)],
        compiler_params=params(16),
        name="place",
    )(meta, slot_wave, *near_parts, *far_arrived, far_got)
    return (columns[None], spectral[None])


def widen_matrix(square):
    levels = square.shape[0]
    pair_eye = jnp.eye(2, dtype=jnp.float32)
    return (square[:, None, :, None] * pair_eye[None, :, None, :]).reshape(2 * levels, 2 * levels)


def per_device_many(fourier, legendre, quad_weights, slot_wave, to_modes, from_modes, mode_rates):
    parity = lax.axis_index("parity")
    signed_one = (1 - 2 * parity).astype(jnp.float32)
    levels = to_modes.shape[0]
    col_width = 2 * levels
    wave_count = slot_wave.shape[0]
    per_owner = legendre.shape[0]
    degrees = legendre.shape[3]
    top_degree = 2 * degrees - 1
    grid_block = fourier[0]
    scaled = (quad_weights[:, None, None] * grid_block.astype(jnp.float32)).astype(jnp.bfloat16)
    scaled = combine(scaled, partner_2(scaled, "parity", 0), signed_one)
    by_slot = jnp.transpose(jnp.take(scaled, slot_wave, axis=1), (1, 0, 2))
    arrived = lax.all_to_all(
        lax.all_to_all(by_slot, "wave", split_axis=0, concat_axis=1, tiled=True),
        "lev",
        split_axis=1,
        concat_axis=2,
        tiled=True,
    )
    owned_waves = lax.dynamic_slice_in_dim(slot_wave, lax.axis_index("wave") * per_owner, per_owner)
    to_wide = widen_matrix(jnp.transpose(to_modes))
    from_wide = widen_matrix(jnp.transpose(from_modes))
    rates_wide = jnp.repeat(mode_rates, 2)
    half_deg = degrees // lax.axis_size("lev")
    pieces = []
    for owned in range(per_owner):
        deg_block = legendre[owned, 0]
        pieces.append(
            lax.dot_general(
                deg_block,
                arrived[owned],
                (((0,), (0,)), ((), ())),
                preferred_element_type=jnp.float32,
            )
        )
    summed = lax.psum(jnp.concatenate(pieces, axis=1), "lev")
    row_count = summed.shape[0]
    degree_idx = jnp.arange(row_count, dtype=jnp.int32)
    degree = (owned_waves[None, :] + 2 * degree_idx[:, None] + parity).reshape(-1, 1)
    flat = summed.reshape(-1, col_width)
    kept = jnp.where(degree <= top_degree, flat, jnp.zeros_like(flat))
    degree_f = degree.astype(jnp.float32)
    stiffness = degree_f * (degree_f + 1.0) / (top_degree * (top_degree + 1.0))
    mode_part = jnp.dot(
        kept, to_wide, precision=lax.Precision.HIGHEST, preferred_element_type=jnp.float32
    )
    mode_part = mode_part / (1.0 + stiffness * rates_wide[None, :])
    updated = jnp.dot(
        mode_part, from_wide, precision=lax.Precision.HIGHEST, preferred_element_type=jnp.float32
    )
    updated = updated.reshape(row_count, per_owner * col_width).astype(jnp.bfloat16)
    sums = []
    for owned in range(per_owner):
        deg_block = legendre[owned, 0]
        coeffs = updated[:, owned * col_width : (owned + 1) * col_width]
        sums.append(jnp.dot(deg_block, coeffs, preferred_element_type=jnp.float32))
    grid_sums = jnp.stack(sums)
    spectral_mine = lax.dynamic_slice_in_dim(updated, lax.axis_index("lev") * half_deg, half_deg, 0)
    parts = grid_sums.astype(jnp.bfloat16)
    returned = lax.all_to_all(
        lax.all_to_all(parts, "lev", split_axis=2, concat_axis=1, tiled=True),
        "wave",
        split_axis=1,
        concat_axis=0,
        tiled=True,
    )
    returned = combine(returned, partner_2(returned, "parity", 0), signed_one)
    inverse_slot = (
        jnp.zeros((wave_count,), jnp.int32)
        .at[slot_wave]
        .set(jnp.arange(wave_count, dtype=jnp.int32))
    )
    columns = jnp.transpose(jnp.take(returned, inverse_slot, axis=0), (1, 0, 2))
    return (columns[None], spectral_mine[None])


def solution(mesh):
    in_specs = (
        P("parity", "wave", None, "lev"),
        P("wave", "parity", "lev", None),
        P("wave"),
        P(),
        P(),
        P(),
        P(),
    )
    out_specs = (P("parity", "wave", None, "lev"), P("parity", "lev", "wave"))
    few = mesh.shape["wave"] in (4, 8, 16) and mesh.shape["lev"] == 2
    return jax.shard_map(
        per_device if few else per_device_many,
        mesh=mesh,
        in_specs=in_specs,
        out_specs=out_specs,
        check_vma=False,
    )
```

```python
import functools

import jax
import jax.numpy as jnp
from jax import lax
from jax.experimental import pallas as pl
from jax.experimental.pallas import tpu as pltpu
from jax.sharding import PartitionSpec as P

AXES = ("wave", "parity", "lev")
VMEM = pl.BlockSpec(memory_space=pltpu.VMEM)
SMEM = pl.BlockSpec(memory_space=pltpu.SMEM)
HBM = pl.BlockSpec(memory_space=pltpu.HBM)
MIB = 1024 * 1024


def partner_2(value, axis, distance):
    mask = 2**distance
    pairs = [(source, source ^ mask) for source in range(lax.axis_size(axis))]
    return lax.ppermute(value, axis, pairs)


def combine(mine_part, partner, signed_one):
    return (partner.astype(jnp.float32) + signed_one * mine_part.astype(jnp.float32)).astype(
        jnp.bfloat16
    )


RAW_STEPS = 1


def mask_plan(owners):
    even = range(owners - 2, -1, -2)
    cores = [
        [mask + (1 - core if step < RAW_STEPS else core) for step, mask in enumerate(even)]
        for core in range(2)
    ]
    return [masks[RAW_STEPS:] for masks in cores], [masks[:RAW_STEPS] for masks in cores]


def swap(value, axis):
    return lax.ppermute(value, axis, [(0, 1), (1, 0)])


def meet(value, masks):
    owners, hemis = lax.axis_size("wave"), lax.axis_size("parity")
    pairs = []
    for wave in range(owners):
        for hemi in range(hemis):
            for core, mask in enumerate(masks):
                if mask:
                    source = (wave * hemis + hemi) * 2 + core
                    target = ((wave ^ mask) * hemis + hemi) * 2 + core
                    pairs.append((source, target))
    return lax.ppermute(value, AXES, pairs)


def here():
    return tuple(lax.axis_index(axis).astype(jnp.int32) for axis in AXES)


def owner_met(masks, index, wave, core):
    return wave ^ jnp.where(core == 0, masks[0][index], masks[1][index])


def fold_with(sign):
    def fold(own, peer):
        return (peer.astype(jnp.float32) + sign * own.astype(jnp.float32)).astype(jnp.bfloat16)

    return fold


def parity_sign(parity):
    return (1 - 2 * parity).astype(jnp.float32)


def join_kernel(mine, got, *outs):
    for i, out in enumerate(outs):
        out[:, 0] = mine[i]
        out[:, 1] = got[i]


def fold_kernel(own, peer, out):
    out[...] = fold_with(parity_sign(here()[1]))(own[...], peer[...])


def gather_kernel(*refs, folds, raws):
    raw, folded, (sent, keep, give) = refs[:raws], refs[raws:-3], refs[-3:]
    lev = here()[2]
    for part, out in enumerate((keep, give)):
        for i in range(folds):
            value = folded[i][part]
            if i == folds - 1:
                value = jnp.where(lev == 0, sent[part], value)
            out[i] = value
        for i in range(raws):
            out[folds + i] = raw[i][part]


def exchange(fold_mine, fold_other, raw_mine, raw_other, aside, plan):
    folds, _, rows, side = fold_mine.shape
    raws = raw_mine.shape[0]
    fold_masks, raw_masks = plan
    block = jax.ShapeDtypeStruct((2, 2, rows, side), jnp.bfloat16)
    fold = call(fold_kernel, block, "fold", 8)
    raw_got = swap(raw_other, "lev")
    fold_got = swap(fold_other, "lev")
    raw_sent = call(join_kernel, (block,) * raws, "join", 8)(raw_mine, raw_got)
    raw = [meet(b, (raw_masks[0][i], raw_masks[1][i])) for i, b in enumerate(raw_sent)]
    raw_folded = [fold(b, swap(b, "parity")) for b in raw]
    aside = aside((fold_got, raw_got))
    plain = call(join_kernel, (block,) * folds, "join", 8)(fold_mine, fold_got)
    sent = [fold(b, swap(b, "parity")) for b in plain]
    folded = [meet(b, (fold_masks[0][i], fold_masks[1][i])) for i, b in enumerate(sent)]
    last, aside = lax.optimization_barrier((sent[-1], aside))
    whole = jax.ShapeDtypeStruct((folds + raws, 2, rows, side), jnp.bfloat16)
    keep, give = call(
        functools.partial(gather_kernel, folds=folds, raws=raws), (whole, whole), "gather", 8
    )(*raw_folded, *folded, last)
    return keep, swap(give, "lev"), aside


def call(kernel, shapes, name, mebibytes, scratch=(), in_specs=None, out_spec=VMEM):
    def run(*args):
        moved = sum(a.size * a.dtype.itemsize for a in (*args, *jax.tree.leaves(shapes)))
        return pl.pallas_call(
            kernel,
            out_shape=shapes,
            in_specs=in_specs or [VMEM] * len(args),
            out_specs=jax.tree.map(lambda _: out_spec, shapes),
            scratch_shapes=scratch,
            cost_estimate=pl.CostEstimate(flops=0, bytes_accessed=moved, transcendentals=0),
            compiler_params=pltpu.CompilerParams(vmem_limit_bytes=mebibytes * MIB),
            name=name,
        )(*args)

    return run


def send_order(plan, wave, lev):
    order = []
    for group, masks in enumerate(plan):
        for i in range(len(masks[0])):
            for other in range(2):
                core = 1 - lev if other else lev
                order.append((2 * group + other, i, owner_met(masks, i, wave, core), core))
    return order


def arrival_order(plan, wave, lev):
    order = []
    for other in range(2):
        core = 1 - lev if other else lev
        at = 0
        for masks in plan:
            for i in range(len(masks[0])):
                order.append((other, at, owner_met(masks, i, wave, core), core))
                at += 1
    return order


def wave_order(slots, waves, group):
    size = waves * group
    row = lax.broadcasted_iota(jnp.int32, (group, size), 0)
    column = lax.broadcasted_iota(jnp.int32, (group, size), 1)
    return jnp.concatenate(
        [(column == row * waves + slots[slot]).astype(jnp.bfloat16) for slot in range(waves)]
    )


def scale_kernel(slots_hbm, grid_hbm, weights_hbm, *refs, plan):
    outs, (slots, grid, weights, wide, held, done) = refs[:4], refs[4:]
    rows, waves, side = grid.shape
    group = wide.shape[0] // waves
    groups = rows // group
    wave, _, lev = here()
    cuts = 2
    step = groups // cuts
    copies = [
        pltpu.make_async_copy(slots_hbm, slots, done.at[0]),
        pltpu.make_async_copy(weights_hbm, weights, done.at[1]),
    ]
    for i in range(cuts):
        at = pl.ds(i * step * group, step * group)
        copies.append(pltpu.make_async_copy(grid_hbm.at[at], grid.at[at], done.at[2 + i]))
    for copy in copies:
        copy.start()
    copies[0].wait()
    order = wave_order(slots, waves, group)
    copies[1].wait()
    scale = jnp.transpose(jnp.broadcast_to(weights[...], (side, rows)))
    for cut in range(cuts):
        copies[2 + cut].wait()
        for i in range(cut * step, (cut + 1) * step):
            wide[:, i * side : (i + 1) * side] = grid[i * group : (i + 1) * group].reshape(
                group * waves, side
            )
        span = slice(cut * step * side, (cut + 1) * step * side)
        picked = jnp.dot(order, wide[:, span], preferred_element_type=jnp.float32)
        for i in range(step):
            at = slice((cut * step + i) * group, (cut * step + i + 1) * group)
            for slot in range(waves):
                held[slot, at] = (
                    scale[at]
                    * picked[slot * group : (slot + 1) * group, i * side : (i + 1) * side]
                ).astype(jnp.bfloat16)
    for out, i, owner, core in send_order(plan, wave, lev):
        outs[out][i, 0] = held[2 * owner + core]
        outs[out][i, 1] = held[2 * owner + 1 - core]


def lanes(index, side):
    return pl.ds(pl.multiple_of(index * side, side), side)


def widen_kernel(to_modes, from_modes, rates, to_wide, from_wide, rate):
    levels = to_modes.shape[0]
    width = 2 * levels
    bf16, f32 = jnp.bfloat16, jnp.float32
    spread = (
        (lax.broadcasted_iota(jnp.int32, (width, levels), 0) >> 1)
        == lax.broadcasted_iota(jnp.int32, (width, levels), 1)
    ).astype(f32)
    spread_16 = spread.astype(bf16)
    row = lax.broadcasted_iota(jnp.int32, (width, width), 0)
    column = lax.broadcasted_iota(jnp.int32, (width, width), 1)
    same = ((row + column) & 1) == 0

    def widen(square):
        tall = jnp.dot(spread_16, square, preferred_element_type=f32).astype(bf16)
        wide = lax.dot_general(
            tall, spread_16, (((1,), (1,)), ((), ())), preferred_element_type=f32
        )
        return jnp.where(same, wide, 0.0).astype(bf16)

    for square, out in ((to_modes, to_wide), (from_modes, from_wide)):
        high = square[...].astype(bf16)
        low = (square[...] - high.astype(f32)).astype(bf16)
        wide = widen(high)
        out[:, 0:width] = wide
        out[:, width : 2 * width] = wide
        out[:, 2 * width :] = widen(low)
    rate[...] = jnp.sum(spread * rates[...], axis=1, keepdims=True)


def product_3(wide, value):
    high = value.astype(jnp.bfloat16)
    low = (value - high.astype(jnp.float32)).astype(jnp.bfloat16)
    return jnp.dot(
        wide[...], jnp.concatenate([high, low, high], axis=0), preferred_element_type=jnp.float32
    )


def solve_kernel(
    slots, keep, got, tables_mine, tables_other, to_wide, from_wide, rate, *refs, plan
):
    (spec_mine, spec_other), outs, (data, spec, parts) = refs[:2], refs[2:6], refs[6:]
    wave, parity, lev = here()
    rows, side = keep.shape[2:]
    half, degrees = tables_mine.shape[2:]
    table_mine, table_other = tables_mine.at[lev, 0], tables_other.at[lev, 0]

    def place(owner):
        return pl.ds(pl.multiple_of(owner * rows, 16), rows)

    for other, index, owner, core in arrival_order(plan, wave, lev):
        block = got if other else keep
        data[place(owner), lanes(core, side)] = block[index, 0]
        data[place(owner), lanes(1 - core, side)] = block[index, 1]
    at_mine = pl.ds(pl.multiple_of(lev * half, 16), half)
    at_other = pl.ds(pl.multiple_of((1 - lev) * half, 16), half)
    rows_first = (((0,), (0,)), ((), ()))
    raw = lax.dot_general(
        data[at_mine, :], table_mine[...], rows_first, preferred_element_type=jnp.float32
    ) + lax.dot_general(
        data[at_other, :], table_other[...], rows_first, preferred_element_type=jnp.float32
    )
    top_degree = 2 * degrees - 1
    degree = (
        slots[2 * wave + lev] + parity + 2 * lax.broadcasted_iota(jnp.int32, (1, degrees), 1)
    )
    kept = jnp.where(degree <= top_degree, raw, 0.0)
    degree_f = degree.astype(jnp.float32)
    stiffness = degree_f * (degree_f + 1.0) / (top_degree * (top_degree + 1.0))
    damped = product_3(to_wide, kept) / (1.0 + stiffness * rate[...])
    updated = product_3(from_wide, damped)
    spec[...] = jnp.transpose(updated.astype(jnp.bfloat16))
    for at, table in ((at_mine, table_mine), (at_other, table_other)):
        parts[at, :] = jnp.dot(
            table[...], spec[...], preferred_element_type=jnp.float32
        ).astype(jnp.bfloat16)
    spec_mine[...] = spec[at_mine, :]
    spec_other[...] = spec[at_other, :]
    for out, i, owner, core in send_order(plan, wave, lev):
        outs[out][i, 0] = parts[place(owner), lanes(core, side)]
        outs[out][i, 1] = parts[place(owner), lanes(1 - core, side)]


def place_kernel(slots, keep, got, spec_mine, spec_got, columns, spectral, *refs, plan):
    held, wide, ready, done = refs
    rows, waves, side = ready.shape
    group = wide.shape[0] // waves
    groups = rows // group
    wave, _, lev = here()
    width = spec_mine.shape[1]
    copies = [
        pltpu.make_async_copy(half, spectral.at[:, lanes(core, width)], done.at[i])
        for i, (half, core) in enumerate(((spec_mine, lev), (spec_got, 1 - lev)))
    ]
    for copy in copies:
        copy.start()
    for other, index, owner, core in arrival_order(plan, wave, lev):
        block = got if other else keep
        held[2 * owner + core] = block[index, 0]
        held[2 * owner + 1 - core] = block[index, 1]
    order = wave_order(slots, waves, group)
    cuts = done.shape[0] - 2
    step = groups // cuts
    for cut in range(cuts):
        for i in range(cut * step, (cut + 1) * step):
            for slot in range(waves):
                wide[slot * group : (slot + 1) * group, i * side : (i + 1) * side] = held[
                    slot, i * group : (i + 1) * group
                ]
        span = slice(cut * step * side, (cut + 1) * step * side)
        placed = lax.dot_general(
            order,
            wide[:, span],
            (((0,), (0,)), ((), ())),
            preferred_element_type=jnp.float32,
        ).astype(jnp.bfloat16)
        for i in range(step):
            ready[(cut * step + i) * group : (cut * step + i + 1) * group] = placed[
                :, i * side : (i + 1) * side
            ].reshape(group, waves, side)
        at = pl.ds(cut * step * group, step * group)
        copies.append(pltpu.make_async_copy(ready.at[at], columns.at[at], done.at[2 + cut]))
        copies[-1].start()
    for copy in copies:
        copy.wait()


def per_device(fourier, legendre, quad_weights, slot_wave, to_modes, from_modes, mode_rates):
    plan = mask_plan(lax.axis_size("wave"))
    rows, waves, side = fourier.shape[1:]
    width = 2 * side
    half, degrees = legendre.shape[2:]
    bf16, f32 = jnp.bfloat16, jnp.float32
    pieces = tuple(
        jax.ShapeDtypeStruct((len(masks[0]), 2, rows, side), bf16) for masks in plan for _ in range(2)
    )
    group = 16
    held = pltpu.VMEM((waves, rows, side), bf16)
    wide_rows = pltpu.VMEM((group * waves, rows // group * side), bf16)

    scaled = call(
        functools.partial(scale_kernel, plan=plan),
        pieces,
        "scale",
        48,
        (
            pltpu.SMEM(slot_wave.shape, jnp.int32),
            pltpu.VMEM((rows, waves, side), bf16),
            pltpu.VMEM((1, rows), f32),
            wide_rows,
            held,
            pltpu.SemaphoreType.DMA((4,)),
        ),
        [HBM] * 3,
    )(slot_wave, fourier[0], quad_weights[None, :])
    keep, got, table_other = exchange(
        *scaled, lambda tie: swap(lax.optimization_barrier((legendre, *tie))[0], "lev"), plan
    )

    wide = jax.ShapeDtypeStruct((width, 3 * width), bf16)
    to_wide, from_wide, rate = call(
        widen_kernel, (wide, wide, jax.ShapeDtypeStruct((width, 1), f32)), "widen", 8
    )(to_modes, from_modes, mode_rates[None, :])
    spec_shape = jax.ShapeDtypeStruct((half, width), bf16)
    spec_mine, spec_other, *parts = call(
        functools.partial(solve_kernel, plan=plan),
        (spec_shape, spec_shape) + pieces,
        "solve",
        20,
        (pltpu.VMEM((2 * half, width), bf16),) * 3,
        [SMEM] + [VMEM] * 7,
    )(slot_wave, keep, got, legendre, table_other, to_wide, from_wide, rate)
    def swap_spectral(tie):
        return swap(lax.optimization_barrier((spec_other, *tie))[0], "lev")

    keep, got, spec_got = exchange(*parts, swap_spectral, plan)
    columns, spectral = call(
        functools.partial(place_kernel, plan=plan),
        (
            jax.ShapeDtypeStruct((rows, waves, side), bf16),
            jax.ShapeDtypeStruct((half, 2 * width), bf16),
        ),
        "place",
        16,
        (
            held,
            wide_rows,
            pltpu.VMEM((rows, waves, side), bf16),
            pltpu.SemaphoreType.DMA((7,)),
        ),
        [SMEM] + [VMEM] * 4,
        HBM,
    )(slot_wave, keep, got, spec_mine, spec_got)
    return (columns[None], spectral[None])


def widen_matrix(square):
    levels = square.shape[0]
    pair_eye = jnp.eye(2, dtype=jnp.float32)
    return (square[:, None, :, None] * pair_eye[None, :, None, :]).reshape(2 * levels, 2 * levels)


def per_device_many(fourier, legendre, quad_weights, slot_wave, to_modes, from_modes, mode_rates):
    parity = lax.axis_index("parity")
    signed_one = (1 - 2 * parity).astype(jnp.float32)
    levels = to_modes.shape[0]
    col_width = 2 * levels
    wave_count = slot_wave.shape[0]
    per_owner = legendre.shape[0]
    degrees = legendre.shape[3]
    top_degree = 2 * degrees - 1
    grid_block = fourier[0]
    scaled = (quad_weights[:, None, None] * grid_block.astype(jnp.float32)).astype(jnp.bfloat16)
    scaled = combine(scaled, partner_2(scaled, "parity", 0), signed_one)
    by_slot = jnp.transpose(jnp.take(scaled, slot_wave, axis=1), (1, 0, 2))
    arrived = lax.all_to_all(
        lax.all_to_all(by_slot, "wave", split_axis=0, concat_axis=1, tiled=True),
        "lev",
        split_axis=1,
        concat_axis=2,
        tiled=True,
    )
    owned_waves = lax.dynamic_slice_in_dim(slot_wave, lax.axis_index("wave") * per_owner, per_owner)
    to_wide = widen_matrix(jnp.transpose(to_modes))
    from_wide = widen_matrix(jnp.transpose(from_modes))
    rates_wide = jnp.repeat(mode_rates, 2)
    half_deg = degrees // lax.axis_size("lev")
    pieces = []
    for owned in range(per_owner):
        deg_block = legendre[owned, 0]
        pieces.append(
            lax.dot_general(
                deg_block,
                arrived[owned],
                (((0,), (0,)), ((), ())),
                preferred_element_type=jnp.float32,
            )
        )
    summed = lax.psum(jnp.concatenate(pieces, axis=1), "lev")
    row_count = summed.shape[0]
    degree_idx = jnp.arange(row_count, dtype=jnp.int32)
    degree = (owned_waves[None, :] + 2 * degree_idx[:, None] + parity).reshape(-1, 1)
    flat = summed.reshape(-1, col_width)
    kept = jnp.where(degree <= top_degree, flat, jnp.zeros_like(flat))
    degree_f = degree.astype(jnp.float32)
    stiffness = degree_f * (degree_f + 1.0) / (top_degree * (top_degree + 1.0))
    mode_part = jnp.dot(
        kept, to_wide, precision=lax.Precision.HIGHEST, preferred_element_type=jnp.float32
    )
    mode_part = mode_part / (1.0 + stiffness * rates_wide[None, :])
    updated = jnp.dot(
        mode_part, from_wide, precision=lax.Precision.HIGHEST, preferred_element_type=jnp.float32
    )
    updated = updated.reshape(row_count, per_owner * col_width).astype(jnp.bfloat16)
    sums = []
    for owned in range(per_owner):
        deg_block = legendre[owned, 0]
        coeffs = updated[:, owned * col_width : (owned + 1) * col_width]
        sums.append(jnp.dot(deg_block, coeffs, preferred_element_type=jnp.float32))
    grid_sums = jnp.stack(sums)
    spectral_mine = lax.dynamic_slice_in_dim(updated, lax.axis_index("lev") * half_deg, half_deg, 0)
    parts = grid_sums.astype(jnp.bfloat16)
    returned = lax.all_to_all(
        lax.all_to_all(parts, "lev", split_axis=2, concat_axis=1, tiled=True),
        "wave",
        split_axis=1,
        concat_axis=0,
        tiled=True,
    )
    returned = combine(returned, partner_2(returned, "parity", 0), signed_one)
    inverse_slot = (
        jnp.zeros((wave_count,), jnp.int32)
        .at[slot_wave]
        .set(jnp.arange(wave_count, dtype=jnp.int32))
    )
    columns = jnp.transpose(jnp.take(returned, inverse_slot, axis=0), (1, 0, 2))
    return (columns[None], spectral_mine[None])


def solution(mesh):
    in_specs = (
        P("parity", "wave", None, "lev"),
        P("wave", "parity", "lev", None),
        P("wave"),
        P(),
        P(),
        P(),
        P(),
    )
    out_specs = (P("parity", "wave", None, "lev"), P("parity", "lev", "wave"))
    few = mesh.shape["wave"] in (8, 16) and mesh.shape["lev"] == mesh.shape["parity"] == 2
    return jax.shard_map(
        per_device if few else per_device_many,
        mesh=mesh,
        in_specs=in_specs,
        out_specs=out_specs,
        check_vma=False,
    )
```

```python
import functools

import jax
import jax.numpy as jnp
from jax import lax
from jax.experimental import pallas as pl
from jax.experimental.pallas import tpu as pltpu
from jax.sharding import PartitionSpec as P

AXES = ("wave", "parity", "lev")
VMEM = pl.BlockSpec(memory_space=pltpu.VMEM)
SMEM = pl.BlockSpec(memory_space=pltpu.SMEM)
HBM = pl.BlockSpec(memory_space=pltpu.HBM)
MIB = 1024 * 1024


def partner_2(value, axis, distance):
    mask = 2**distance
    pairs = [(source, source ^ mask) for source in range(lax.axis_size(axis))]
    return lax.ppermute(value, axis, pairs)


def combine(mine_part, partner, signed_one):
    return (partner.astype(jnp.float32) + signed_one * mine_part.astype(jnp.float32)).astype(
        jnp.bfloat16
    )


def mask_plan(owners):
    middle = owners // 2
    fold, raw = [], []
    for core in range(2):
        far = [
            even + (i + 1 + core) % 2 for i, even in enumerate(range(owners - 2, middle - 1, -2))
        ]
        first = core * middle // 2
        near = list(range(first + middle // 2 - 1, first - 1, -1))
        raw.append(far[0::2] + near[0::2])
        fold.append(far[1::2] + near[1::2])
    return fold, raw


def swap(value, axis):
    return lax.ppermute(value, axis, [(0, 1), (1, 0)])


def meet(value, masks):
    owners, hemis = lax.axis_size("wave"), lax.axis_size("parity")
    pairs = []
    for wave in range(owners):
        for hemi in range(hemis):
            for core, mask in enumerate(masks):
                if mask:
                    source = (wave * hemis + hemi) * 2 + core
                    target = ((wave ^ mask) * hemis + hemi) * 2 + core
                    pairs.append((source, target))
    return lax.ppermute(value, AXES, pairs)


def here():
    return tuple(lax.axis_index(axis).astype(jnp.int32) for axis in AXES)


def owner_met(masks, index, wave, core):
    return wave ^ jnp.where(core == 0, masks[0][index], masks[1][index])


def fold_with(sign):
    def fold(own, peer):
        return (peer.astype(jnp.float32) + sign * own.astype(jnp.float32)).astype(jnp.bfloat16)

    return fold


def parity_sign(parity):
    return (1 - 2 * parity).astype(jnp.float32)


def join_kernel(mine, got, *outs):
    for i, out in enumerate(outs):
        out[:, 0] = mine[i]
        out[:, 1] = got[i]


def fold_kernel(own, peer, out):
    out[...] = fold_with(parity_sign(here()[1]))(own[...], peer[...])


def gather_kernel(*refs, folds, raws):
    raw, folded, (sent, keep, give) = refs[:raws], refs[raws:-3], refs[-3:]
    lev = here()[2]
    for part, out in enumerate((keep, give)):
        for i in range(folds):
            value = folded[i][part]
            if i == folds - 1:
                value = jnp.where(lev == 0, sent[part], value)
            out[i] = value
        for i in range(raws):
            out[folds + i] = raw[i][part]


def exchange(fold_mine, fold_other, raw_mine, raw_other, aside, plan):
    folds, _, rows, side = fold_mine.shape
    raws = raw_mine.shape[0]
    fold_masks, raw_masks = plan
    block = jax.ShapeDtypeStruct((2, 2, rows, side), jnp.bfloat16)
    fold = call(fold_kernel, block, "fold", 8)
    raw_got = swap(raw_other, "lev")
    fold_got = swap(fold_other, "lev")
    raw_sent = call(join_kernel, (block,) * raws, "join", 8)(raw_mine, raw_got)
    raw = [meet(b, (raw_masks[0][i], raw_masks[1][i])) for i, b in enumerate(raw_sent)]
    raw_peer = [swap(b, "parity") for b in raw]
    aside = aside((fold_got, raw_got))
    plain = call(join_kernel, (block,) * folds, "join", 8)(fold_mine, fold_got)
    sent = [fold(b, swap(b, "parity")) for b in plain]
    folded = [meet(b, (fold_masks[0][i], fold_masks[1][i])) for i, b in enumerate(sent)]
    raw_peer[0] = lax.optimization_barrier((raw_peer[0], folded[0]))[0]
    raw_folded = [fold(b, peer) for b, peer in zip(raw, raw_peer)]
    last, aside = lax.optimization_barrier((sent[-1], aside))
    whole = jax.ShapeDtypeStruct((folds + raws, 2, rows, side), jnp.bfloat16)
    keep, give = call(
        functools.partial(gather_kernel, folds=folds, raws=raws), (whole, whole), "gather", 8
    )(*raw_folded, *folded, last)
    return keep, swap(give, "lev"), aside


def call(kernel, shapes, name, mebibytes, scratch=(), in_specs=None, out_spec=VMEM):
    def run(*args):
        moved = sum(a.size * a.dtype.itemsize for a in (*args, *jax.tree.leaves(shapes)))
        return pl.pallas_call(
            kernel,
            out_shape=shapes,
            in_specs=in_specs or [VMEM] * len(args),
            out_specs=jax.tree.map(lambda _: out_spec, shapes),
            scratch_shapes=scratch,
            cost_estimate=pl.CostEstimate(flops=0, bytes_accessed=moved, transcendentals=0),
            compiler_params=pltpu.CompilerParams(vmem_limit_bytes=mebibytes * MIB),
            name=name,
        )(*args)

    return run


def send_order(plan, wave, lev):
    order = []
    for group, masks in enumerate(plan):
        for i in range(len(masks[0])):
            for other in range(2):
                core = 1 - lev if other else lev
                order.append((2 * group + other, i, owner_met(masks, i, wave, core), core))
    return order


def arrival_order(plan, wave, lev):
    order = []
    for other in range(2):
        core = 1 - lev if other else lev
        at = 0
        for masks in plan:
            for i in range(len(masks[0])):
                order.append((other, at, owner_met(masks, i, wave, core), core))
                at += 1
    return order


def wave_order(slots, waves, group):
    size = waves * group
    row = lax.broadcasted_iota(jnp.int32, (group, size), 0)
    column = lax.broadcasted_iota(jnp.int32, (group, size), 1)
    return jnp.concatenate(
        [(column == row * waves + slots[slot]).astype(jnp.bfloat16) for slot in range(waves)]
    )


def scale_kernel(slots_hbm, grid_hbm, weights_hbm, *refs, plan):
    outs, (slots, grid, weights, wide, held, done) = refs[:4], refs[4:]
    rows, waves, side = grid.shape
    group = wide.shape[0] // waves
    groups = rows // group
    wave, _, lev = here()
    cuts = 2
    step = groups // cuts
    copies = [
        pltpu.make_async_copy(slots_hbm, slots, done.at[0]),
        pltpu.make_async_copy(weights_hbm, weights, done.at[1]),
    ]
    for i in range(cuts):
        at = pl.ds(i * step * group, step * group)
        copies.append(pltpu.make_async_copy(grid_hbm.at[at], grid.at[at], done.at[2 + i]))
    for copy in copies:
        copy.start()
    copies[0].wait()
    order = wave_order(slots, waves, group)
    copies[1].wait()
    scale = jnp.transpose(jnp.broadcast_to(weights[...], (side, rows)))
    for cut in range(cuts):
        copies[2 + cut].wait()
        for i in range(cut * step, (cut + 1) * step):
            wide[:, i * side : (i + 1) * side] = grid[i * group : (i + 1) * group].reshape(
                group * waves, side
            )
        span = slice(cut * step * side, (cut + 1) * step * side)
        picked = jnp.dot(order, wide[:, span], preferred_element_type=jnp.float32)
        for i in range(step):
            at = slice((cut * step + i) * group, (cut * step + i + 1) * group)
            for slot in range(waves):
                held[slot, at] = (
                    scale[at]
                    * picked[slot * group : (slot + 1) * group, i * side : (i + 1) * side]
                ).astype(jnp.bfloat16)
    for out, i, owner, core in send_order(plan, wave, lev):
        outs[out][i, 0] = held[2 * owner + core]
        outs[out][i, 1] = held[2 * owner + 1 - core]


def lanes(index, side):
    return pl.ds(pl.multiple_of(index * side, side), side)


def widen_kernel(to_modes, from_modes, rates, to_wide, from_wide, rate):
    levels = to_modes.shape[0]
    width = 2 * levels
    bf16, f32 = jnp.bfloat16, jnp.float32
    spread = (
        (lax.broadcasted_iota(jnp.int32, (width, levels), 0) >> 1)
        == lax.broadcasted_iota(jnp.int32, (width, levels), 1)
    ).astype(f32)
    spread_16 = spread.astype(bf16)
    row = lax.broadcasted_iota(jnp.int32, (width, width), 0)
    column = lax.broadcasted_iota(jnp.int32, (width, width), 1)
    same = ((row + column) & 1) == 0

    def widen(square):
        tall = jnp.dot(spread_16, square, preferred_element_type=f32).astype(bf16)
        wide = lax.dot_general(
            tall, spread_16, (((1,), (1,)), ((), ())), preferred_element_type=f32
        )
        return jnp.where(same, wide, 0.0).astype(bf16)

    for square, out in ((to_modes, to_wide), (from_modes, from_wide)):
        high = square[...].astype(bf16)
        low = (square[...] - high.astype(f32)).astype(bf16)
        wide = widen(high)
        out[:, 0:width] = wide
        out[:, width : 2 * width] = wide
        out[:, 2 * width :] = widen(low)
    rate[...] = jnp.sum(spread * rates[...], axis=1, keepdims=True)


def product_3(wide, value):
    high = value.astype(jnp.bfloat16)
    low = (value - high.astype(jnp.float32)).astype(jnp.bfloat16)
    return jnp.dot(
        wide[...], jnp.concatenate([high, low, high], axis=0), preferred_element_type=jnp.float32
    )


def solve_kernel(
    slots, keep, got, tables_mine, tables_other, to_wide, from_wide, rate, *refs, plan
):
    (spec_mine, spec_other), outs, (data, spec, parts) = refs[:2], refs[2:6], refs[6:]
    wave, parity, lev = here()
    rows, side = keep.shape[2:]
    half, degrees = tables_mine.shape[2:]
    table_mine, table_other = tables_mine.at[lev, 0], tables_other.at[lev, 0]

    def place(owner):
        return pl.ds(pl.multiple_of(owner * rows, 16), rows)

    for other, index, owner, core in arrival_order(plan, wave, lev):
        block = got if other else keep
        data[place(owner), lanes(core, side)] = block[index, 0]
        data[place(owner), lanes(1 - core, side)] = block[index, 1]
    at_mine = pl.ds(pl.multiple_of(lev * half, 16), half)
    at_other = pl.ds(pl.multiple_of((1 - lev) * half, 16), half)
    rows_first = (((0,), (0,)), ((), ()))
    raw = lax.dot_general(
        data[at_mine, :], table_mine[...], rows_first, preferred_element_type=jnp.float32
    ) + lax.dot_general(
        data[at_other, :], table_other[...], rows_first, preferred_element_type=jnp.float32
    )
    top_degree = 2 * degrees - 1
    degree = (
        slots[2 * wave + lev] + parity + 2 * lax.broadcasted_iota(jnp.int32, (1, degrees), 1)
    )
    kept = jnp.where(degree <= top_degree, raw, 0.0)
    degree_f = degree.astype(jnp.float32)
    stiffness = degree_f * (degree_f + 1.0) / (top_degree * (top_degree + 1.0))
    damped = product_3(to_wide, kept) / (1.0 + stiffness * rate[...])
    updated = product_3(from_wide, damped)
    spec[...] = jnp.transpose(updated.astype(jnp.bfloat16))
    for at, table in ((at_mine, table_mine), (at_other, table_other)):
        parts[at, :] = jnp.dot(
            table[...], spec[...], preferred_element_type=jnp.float32
        ).astype(jnp.bfloat16)
    spec_mine[...] = spec[at_mine, :]
    spec_other[...] = spec[at_other, :]
    for out, i, owner, core in send_order(plan, wave, lev):
        outs[out][i, 0] = parts[place(owner), lanes(core, side)]
        outs[out][i, 1] = parts[place(owner), lanes(1 - core, side)]


def place_kernel(slots, keep, got, spec_mine, spec_got, columns, spectral, *refs, plan):
    held, wide, ready, done = refs
    rows, waves, side = ready.shape
    group = wide.shape[0] // waves
    groups = rows // group
    wave, _, lev = here()
    width = spec_mine.shape[1]
    copies = [
        pltpu.make_async_copy(half, spectral.at[:, lanes(core, width)], done.at[i])
        for i, (half, core) in enumerate(((spec_mine, lev), (spec_got, 1 - lev)))
    ]
    for copy in copies:
        copy.start()
    for other, index, owner, core in arrival_order(plan, wave, lev):
        block = got if other else keep
        held[2 * owner + core] = block[index, 0]
        held[2 * owner + 1 - core] = block[index, 1]
    order = wave_order(slots, waves, group)
    cuts = done.shape[0] - 2
    step = groups // cuts
    for cut in range(cuts):
        for i in range(cut * step, (cut + 1) * step):
            for slot in range(waves):
                wide[slot * group : (slot + 1) * group, i * side : (i + 1) * side] = held[
                    slot, i * group : (i + 1) * group
                ]
        span = slice(cut * step * side, (cut + 1) * step * side)
        placed = lax.dot_general(
            order,
            wide[:, span],
            (((0,), (0,)), ((), ())),
            preferred_element_type=jnp.float32,
        ).astype(jnp.bfloat16)
        for i in range(step):
            ready[(cut * step + i) * group : (cut * step + i + 1) * group] = placed[
                :, i * side : (i + 1) * side
            ].reshape(group, waves, side)
        at = pl.ds(cut * step * group, step * group)
        copies.append(pltpu.make_async_copy(ready.at[at], columns.at[at], done.at[2 + cut]))
        copies[-1].start()
    for copy in copies:
        copy.wait()


def per_device(fourier, legendre, quad_weights, slot_wave, to_modes, from_modes, mode_rates):
    plan = mask_plan(lax.axis_size("wave"))
    rows, waves, side = fourier.shape[1:]
    width = 2 * side
    half, degrees = legendre.shape[2:]
    bf16, f32 = jnp.bfloat16, jnp.float32
    pieces = tuple(
        jax.ShapeDtypeStruct((len(masks[0]), 2, rows, side), bf16) for masks in plan for _ in range(2)
    )
    group = 16
    held = pltpu.VMEM((waves, rows, side), bf16)
    wide_rows = pltpu.VMEM((group * waves, rows // group * side), bf16)

    scaled = call(
        functools.partial(scale_kernel, plan=plan),
        pieces,
        "scale",
        48,
        (
            pltpu.SMEM(slot_wave.shape, jnp.int32),
            pltpu.VMEM((rows, waves, side), bf16),
            pltpu.VMEM((1, rows), f32),
            wide_rows,
            held,
            pltpu.SemaphoreType.DMA((4,)),
        ),
        [HBM] * 3,
    )(slot_wave, fourier[0], quad_weights[None, :])
    keep, got, table_other = exchange(
        *scaled, lambda tie: swap(lax.optimization_barrier((legendre, *tie))[0], "lev"), plan
    )

    wide = jax.ShapeDtypeStruct((width, 3 * width), bf16)
    to_wide, from_wide, rate = call(
        widen_kernel, (wide, wide, jax.ShapeDtypeStruct((width, 1), f32)), "widen", 8
    )(to_modes, from_modes, mode_rates[None, :])
    spec_shape = jax.ShapeDtypeStruct((half, width), bf16)
    spec_mine, spec_other, *parts = call(
        functools.partial(solve_kernel, plan=plan),
        (spec_shape, spec_shape) + pieces,
        "solve",
        20,
        (pltpu.VMEM((2 * half, width), bf16),) * 3,
        [SMEM] + [VMEM] * 7,
    )(slot_wave, keep, got, legendre, table_other, to_wide, from_wide, rate)
    def swap_spectral(tie):
        return swap(lax.optimization_barrier((spec_other, *tie))[0], "lev")

    keep, got, spec_got = exchange(*parts, swap_spectral, plan)
    columns, spectral = call(
        functools.partial(place_kernel, plan=plan),
        (
            jax.ShapeDtypeStruct((rows, waves, side), bf16),
            jax.ShapeDtypeStruct((half, 2 * width), bf16),
        ),
        "place",
        16,
        (
            held,
            wide_rows,
            pltpu.VMEM((rows, waves, side), bf16),
            pltpu.SemaphoreType.DMA((7,)),
        ),
        [SMEM] + [VMEM] * 4,
        HBM,
    )(slot_wave, keep, got, spec_mine, spec_got)
    return (columns[None], spectral[None])


def widen_matrix(square):
    levels = square.shape[0]
    pair_eye = jnp.eye(2, dtype=jnp.float32)
    return (square[:, None, :, None] * pair_eye[None, :, None, :]).reshape(2 * levels, 2 * levels)


def per_device_many(fourier, legendre, quad_weights, slot_wave, to_modes, from_modes, mode_rates):
    parity = lax.axis_index("parity")
    signed_one = (1 - 2 * parity).astype(jnp.float32)
    levels = to_modes.shape[0]
    col_width = 2 * levels
    wave_count = slot_wave.shape[0]
    per_owner = legendre.shape[0]
    degrees = legendre.shape[3]
    top_degree = 2 * degrees - 1
    grid_block = fourier[0]
    scaled = (quad_weights[:, None, None] * grid_block.astype(jnp.float32)).astype(jnp.bfloat16)
    scaled = combine(scaled, partner_2(scaled, "parity", 0), signed_one)
    by_slot = jnp.transpose(jnp.take(scaled, slot_wave, axis=1), (1, 0, 2))
    arrived = lax.all_to_all(
        lax.all_to_all(by_slot, "wave", split_axis=0, concat_axis=1, tiled=True),
        "lev",
        split_axis=1,
        concat_axis=2,
        tiled=True,
    )
    owned_waves = lax.dynamic_slice_in_dim(slot_wave, lax.axis_index("wave") * per_owner, per_owner)
    to_wide = widen_matrix(jnp.transpose(to_modes))
    from_wide = widen_matrix(jnp.transpose(from_modes))
    rates_wide = jnp.repeat(mode_rates, 2)
    half_deg = degrees // lax.axis_size("lev")
    pieces = []
    for owned in range(per_owner):
        deg_block = legendre[owned, 0]
        pieces.append(
            lax.dot_general(
                deg_block,
                arrived[owned],
                (((0,), (0,)), ((), ())),
                preferred_element_type=jnp.float32,
            )
        )
    summed = lax.psum(jnp.concatenate(pieces, axis=1), "lev")
    row_count = summed.shape[0]
    degree_idx = jnp.arange(row_count, dtype=jnp.int32)
    degree = (owned_waves[None, :] + 2 * degree_idx[:, None] + parity).reshape(-1, 1)
    flat = summed.reshape(-1, col_width)
    kept = jnp.where(degree <= top_degree, flat, jnp.zeros_like(flat))
    degree_f = degree.astype(jnp.float32)
    stiffness = degree_f * (degree_f + 1.0) / (top_degree * (top_degree + 1.0))
    mode_part = jnp.dot(
        kept, to_wide, precision=lax.Precision.HIGHEST, preferred_element_type=jnp.float32
    )
    mode_part = mode_part / (1.0 + stiffness * rates_wide[None, :])
    updated = jnp.dot(
        mode_part, from_wide, precision=lax.Precision.HIGHEST, preferred_element_type=jnp.float32
    )
    updated = updated.reshape(row_count, per_owner * col_width).astype(jnp.bfloat16)
    sums = []
    for owned in range(per_owner):
        deg_block = legendre[owned, 0]
        coeffs = updated[:, owned * col_width : (owned + 1) * col_width]
        sums.append(jnp.dot(deg_block, coeffs, preferred_element_type=jnp.float32))
    grid_sums = jnp.stack(sums)
    spectral_mine = lax.dynamic_slice_in_dim(updated, lax.axis_index("lev") * half_deg, half_deg, 0)
    parts = grid_sums.astype(jnp.bfloat16)
    returned = lax.all_to_all(
        lax.all_to_all(parts, "lev", split_axis=2, concat_axis=1, tiled=True),
        "wave",
        split_axis=1,
        concat_axis=0,
        tiled=True,
    )
    returned = combine(returned, partner_2(returned, "parity", 0), signed_one)
    inverse_slot = (
        jnp.zeros((wave_count,), jnp.int32)
        .at[slot_wave]
        .set(jnp.arange(wave_count, dtype=jnp.int32))
    )
    columns = jnp.transpose(jnp.take(returned, inverse_slot, axis=0), (1, 0, 2))
    return (columns[None], spectral_mine[None])


def solution(mesh):
    in_specs = (
        P("parity", "wave", None, "lev"),
        P("wave", "parity", "lev", None),
        P("wave"),
        P(),
        P(),
        P(),
        P(),
    )
    out_specs = (P("parity", "wave", None, "lev"), P("parity", "lev", "wave"))
    few = mesh.shape["wave"] in (8, 16) and mesh.shape["lev"] == mesh.shape["parity"] == 2
    return jax.shard_map(
        per_device if few else per_device_many,
        mesh=mesh,
        in_specs=in_specs,
        out_specs=out_specs,
        check_vma=False,
    )
```

```python
import functools

import jax
import jax.numpy as jnp
from jax import lax
from jax.experimental import pallas as pl
from jax.experimental.pallas import tpu as pltpu
from jax.sharding import PartitionSpec as P

AXES = ("wave", "parity", "lev")
VMEM = pl.BlockSpec(memory_space=pltpu.VMEM)
SMEM = pl.BlockSpec(memory_space=pltpu.SMEM)
HBM = pl.BlockSpec(memory_space=pltpu.HBM)
MIB = 1024 * 1024


def partner_2(value, axis, distance):
    mask = 2**distance
    pairs = [(source, source ^ mask) for source in range(lax.axis_size(axis))]
    return lax.ppermute(value, axis, pairs)


def combine(mine_part, partner, signed_one):
    return (partner.astype(jnp.float32) + signed_one * mine_part.astype(jnp.float32)).astype(
        jnp.bfloat16
    )


def mask_plan(owners):
    middle = owners // 2
    fold, raw = [], []
    for core in range(2):
        far = [
            even + (i + 1 + core) % 2 for i, even in enumerate(range(owners - 2, middle - 1, -2))
        ]
        first = core * middle // 2
        near = list(range(first + middle // 2 - 1, first - 1, -1))
        raw.append(far[0::2] + near[0::2])
        fold.append(far[1::2] + near[1::2])
    return fold, raw


def swap(value, axis):
    return lax.ppermute(value, axis, [(0, 1), (1, 0)])


def meet(value, masks):
    owners, hemis = lax.axis_size("wave"), lax.axis_size("parity")
    pairs = []
    for wave in range(owners):
        for hemi in range(hemis):
            for core, mask in enumerate(masks):
                if mask:
                    source = (wave * hemis + hemi) * 2 + core
                    target = ((wave ^ mask) * hemis + hemi) * 2 + core
                    pairs.append((source, target))
    return lax.ppermute(value, AXES, pairs)


def here():
    return tuple(lax.axis_index(axis).astype(jnp.int32) for axis in AXES)


def owner_met(masks, index, wave, core):
    return wave ^ jnp.where(core == 0, masks[0][index], masks[1][index])


def fold_with(sign):
    def fold(own, peer):
        return (peer.astype(jnp.float32) + sign * own.astype(jnp.float32)).astype(jnp.bfloat16)

    return fold


def parity_sign(parity):
    return (1 - 2 * parity).astype(jnp.float32)


def join_kernel(mine, got, *outs):
    for i, out in enumerate(outs):
        out[:, 0] = mine[i]
        out[:, 1] = got[i]


def fold_kernel(own, peer, out):
    out[...] = fold_with(parity_sign(here()[1]))(own[...], peer[...])


def gather_kernel(*refs, folds, raws):
    raw, folded, (sent, keep, give) = refs[:raws], refs[raws:-3], refs[-3:]
    lev = here()[2]
    for part, out in enumerate((keep, give)):
        for i in range(folds):
            value = folded[i][part]
            if i == folds - 1:
                value = jnp.where(lev == 0, sent[part], value)
            out[i] = value
        for i in range(raws):
            out[folds + i] = raw[i][part]


def exchange(fold_mine, fold_other, raw_mine, raw_other, aside, plan):
    folds, _, rows, side = fold_mine.shape
    raws = raw_mine.shape[0]
    fold_masks, raw_masks = plan
    block = jax.ShapeDtypeStruct((2, 2, rows, side), jnp.bfloat16)
    fold = call(fold_kernel, block, "fold", 8)
    raw_got = swap(raw_other, "lev")
    fold_got = swap(fold_other, "lev")
    raw_sent = call(join_kernel, (block,) * raws, "join", 8)(raw_mine, raw_got)
    raw = [meet(b, (raw_masks[0][i], raw_masks[1][i])) for i, b in enumerate(raw_sent)]
    raw_peer = [swap(b, "parity") for b in raw]
    aside = aside((fold_got, raw_got))
    plain = call(join_kernel, (block,) * folds, "join", 8)(fold_mine, fold_got)
    sent = [fold(b, swap(b, "parity")) for b in plain]
    folded = [meet(b, (fold_masks[0][i], fold_masks[1][i])) for i, b in enumerate(sent)]
    raw_peer[0] = lax.optimization_barrier((raw_peer[0], folded[0]))[0]
    raw_folded = [fold(b, peer) for b, peer in zip(raw, raw_peer)]
    last, aside = lax.optimization_barrier((sent[-1], aside))
    whole = jax.ShapeDtypeStruct((folds + raws, 2, rows, side), jnp.bfloat16)
    keep, give = call(
        functools.partial(gather_kernel, folds=folds, raws=raws), (whole, whole), "gather", 8
    )(*raw_folded, *folded, last)
    return keep, swap(give, "lev"), aside


def call(kernel, shapes, name, mebibytes, scratch=(), in_specs=None, out_spec=VMEM):
    def run(*args):
        moved = sum(a.size * a.dtype.itemsize for a in (*args, *jax.tree.leaves(shapes)))
        return pl.pallas_call(
            kernel,
            out_shape=shapes,
            in_specs=in_specs or [VMEM] * len(args),
            out_specs=jax.tree.map(lambda _: out_spec, shapes),
            scratch_shapes=scratch,
            cost_estimate=pl.CostEstimate(flops=0, bytes_accessed=moved, transcendentals=0),
            compiler_params=pltpu.CompilerParams(vmem_limit_bytes=mebibytes * MIB),
            name=name,
        )(*args)

    return run


def send_order(plan, wave, lev):
    order = []
    for group, masks in enumerate(plan):
        for i in range(len(masks[0])):
            for other in range(2):
                core = 1 - lev if other else lev
                order.append((2 * group + other, i, owner_met(masks, i, wave, core), core))
    return order


def arrival_order(plan, wave, lev):
    order = []
    for other in range(2):
        core = 1 - lev if other else lev
        at = 0
        for masks in plan:
            for i in range(len(masks[0])):
                order.append((other, at, owner_met(masks, i, wave, core), core))
                at += 1
    return order


def wave_order(slots, waves, group):
    size = waves * group
    row = lax.broadcasted_iota(jnp.int32, (group, size), 0)
    column = lax.broadcasted_iota(jnp.int32, (group, size), 1)
    return jnp.concatenate(
        [(column == row * waves + slots[slot]).astype(jnp.bfloat16) for slot in range(waves)]
    )


def scale_kernel(slots_hbm, grid_hbm, weights_hbm, *refs, plan):
    outs, (slots, grid, weights, wide, held, done) = refs[:4], refs[4:]
    rows, waves, side = grid.shape
    group = wide.shape[0] // waves
    groups = rows // group
    wave, _, lev = here()
    cuts = 2
    step = groups // cuts
    copies = [
        pltpu.make_async_copy(slots_hbm, slots, done.at[0]),
        pltpu.make_async_copy(weights_hbm, weights, done.at[1]),
    ]
    for i in range(cuts):
        at = pl.ds(i * step * group, step * group)
        copies.append(pltpu.make_async_copy(grid_hbm.at[at], grid.at[at], done.at[2 + i]))
    for copy in copies:
        copy.start()
    copies[0].wait()
    order = wave_order(slots, waves, group)
    copies[1].wait()
    scale = jnp.transpose(jnp.broadcast_to(weights[...], (side, rows)))
    for cut in range(cuts):
        copies[2 + cut].wait()
        for i in range(cut * step, (cut + 1) * step):
            wide[:, i * side : (i + 1) * side] = grid[i * group : (i + 1) * group].reshape(
                group * waves, side
            )
        span = slice(cut * step * side, (cut + 1) * step * side)
        picked = jnp.dot(order, wide[:, span], preferred_element_type=jnp.float32)
        for i in range(step):
            at = slice((cut * step + i) * group, (cut * step + i + 1) * group)
            for slot in range(waves):
                held[slot, at] = (
                    scale[at]
                    * picked[slot * group : (slot + 1) * group, i * side : (i + 1) * side]
                ).astype(jnp.bfloat16)
    for out, i, owner, core in send_order(plan, wave, lev):
        outs[out][i, 0] = held[2 * owner + core]
        outs[out][i, 1] = held[2 * owner + 1 - core]


def lanes(index, side):
    return pl.ds(pl.multiple_of(index * side, side), side)


def widen_kernel(to_modes, from_modes, rates, to_wide, from_wide, rate):
    levels = to_modes.shape[0]
    width = 2 * levels
    bf16, f32 = jnp.bfloat16, jnp.float32
    spread = (
        (lax.broadcasted_iota(jnp.int32, (width, levels), 0) >> 1)
        == lax.broadcasted_iota(jnp.int32, (width, levels), 1)
    ).astype(f32)
    spread_16 = spread.astype(bf16)
    row = lax.broadcasted_iota(jnp.int32, (width, width), 0)
    column = lax.broadcasted_iota(jnp.int32, (width, width), 1)
    same = ((row + column) & 1) == 0

    for square, out in ((to_modes, to_wide), (from_modes, from_wide)):
        tall = jnp.dot(spread_16, square[...].astype(bf16), preferred_element_type=f32)
        wide = lax.dot_general(
            tall.astype(bf16), spread_16, (((1,), (1,)), ((), ())), preferred_element_type=f32
        )
        out[...] = jnp.where(same, wide, 0.0).astype(bf16)
    rate[...] = jnp.sum(spread * rates[...], axis=1, keepdims=True)


def solve_kernel(
    slots, keep, got, tables_mine, tables_other, to_wide, from_wide, rate, *refs, plan
):
    (spec_mine, spec_other), outs, (data, spec, parts) = refs[:2], refs[2:6], refs[6:]
    wave, parity, lev = here()
    rows, side = keep.shape[2:]
    half, degrees = tables_mine.shape[2:]
    table_mine, table_other = tables_mine.at[lev, 0], tables_other.at[lev, 0]

    def place(owner):
        return pl.ds(pl.multiple_of(owner * rows, 16), rows)

    for other, index, owner, core in arrival_order(plan, wave, lev):
        block = got if other else keep
        data[place(owner), lanes(core, side)] = block[index, 0]
        data[place(owner), lanes(1 - core, side)] = block[index, 1]
    at_mine = pl.ds(pl.multiple_of(lev * half, 16), half)
    at_other = pl.ds(pl.multiple_of((1 - lev) * half, 16), half)
    rows_first = (((0,), (0,)), ((), ()))
    raw = lax.dot_general(
        data[at_mine, :], table_mine[...], rows_first, preferred_element_type=jnp.float32
    ) + lax.dot_general(
        data[at_other, :], table_other[...], rows_first, preferred_element_type=jnp.float32
    )
    top_degree = 2 * degrees - 1
    degree = (
        slots[2 * wave + lev] + parity + 2 * lax.broadcasted_iota(jnp.int32, (1, degrees), 1)
    )
    kept = jnp.where(degree <= top_degree, raw, 0.0)
    degree_f = degree.astype(jnp.float32)
    stiffness = degree_f * (degree_f + 1.0) / (top_degree * (top_degree + 1.0))
    modal = jnp.dot(to_wide[...], kept.astype(jnp.bfloat16), preferred_element_type=jnp.float32)
    damped = modal / (1.0 + stiffness * rate[...])
    updated = jnp.dot(
        from_wide[...], damped.astype(jnp.bfloat16), preferred_element_type=jnp.float32
    )
    spec[...] = jnp.transpose(updated.astype(jnp.bfloat16))
    for at, table in ((at_mine, table_mine), (at_other, table_other)):
        parts[at, :] = jnp.dot(
            table[...], spec[...], preferred_element_type=jnp.float32
        ).astype(jnp.bfloat16)
    spec_mine[...] = spec[at_mine, :]
    spec_other[...] = spec[at_other, :]
    for out, i, owner, core in send_order(plan, wave, lev):
        outs[out][i, 0] = parts[place(owner), lanes(core, side)]
        outs[out][i, 1] = parts[place(owner), lanes(1 - core, side)]


def place_kernel(slots, keep, got, spec_mine, spec_got, columns, spectral, *refs, plan):
    held, wide, ready, done = refs
    rows, waves, side = ready.shape
    group = wide.shape[0] // waves
    groups = rows // group
    wave, _, lev = here()
    width = spec_mine.shape[1]
    copies = [
        pltpu.make_async_copy(half, spectral.at[:, lanes(core, width)], done.at[i])
        for i, (half, core) in enumerate(((spec_mine, lev), (spec_got, 1 - lev)))
    ]
    for copy in copies:
        copy.start()
    for other, index, owner, core in arrival_order(plan, wave, lev):
        block = got if other else keep
        held[2 * owner + core] = block[index, 0]
        held[2 * owner + 1 - core] = block[index, 1]
    order = wave_order(slots, waves, group)
    cuts = done.shape[0] - 2
    step = groups // cuts
    for cut in range(cuts):
        for i in range(cut * step, (cut + 1) * step):
            for slot in range(waves):
                wide[slot * group : (slot + 1) * group, i * side : (i + 1) * side] = held[
                    slot, i * group : (i + 1) * group
                ]
        span = slice(cut * step * side, (cut + 1) * step * side)
        placed = lax.dot_general(
            order,
            wide[:, span],
            (((0,), (0,)), ((), ())),
            preferred_element_type=jnp.float32,
        ).astype(jnp.bfloat16)
        for i in range(step):
            ready[(cut * step + i) * group : (cut * step + i + 1) * group] = placed[
                :, i * side : (i + 1) * side
            ].reshape(group, waves, side)
        at = pl.ds(cut * step * group, step * group)
        copies.append(pltpu.make_async_copy(ready.at[at], columns.at[at], done.at[2 + cut]))
        copies[-1].start()
    for copy in copies:
        copy.wait()


def per_device(fourier, legendre, quad_weights, slot_wave, to_modes, from_modes, mode_rates):
    plan = mask_plan(lax.axis_size("wave"))
    rows, waves, side = fourier.shape[1:]
    width = 2 * side
    half, degrees = legendre.shape[2:]
    bf16, f32 = jnp.bfloat16, jnp.float32
    pieces = tuple(
        jax.ShapeDtypeStruct((len(masks[0]), 2, rows, side), bf16) for masks in plan for _ in range(2)
    )
    group = 16
    held = pltpu.VMEM((waves, rows, side), bf16)
    wide_rows = pltpu.VMEM((group * waves, rows // group * side), bf16)

    scaled = call(
        functools.partial(scale_kernel, plan=plan),
        pieces,
        "scale",
        48,
        (
            pltpu.SMEM(slot_wave.shape, jnp.int32),
            pltpu.VMEM((rows, waves, side), bf16),
            pltpu.VMEM((1, rows), f32),
            wide_rows,
            held,
            pltpu.SemaphoreType.DMA((4,)),
        ),
        [HBM] * 3,
    )(slot_wave, fourier[0], quad_weights[None, :])
    keep, got, table_other = exchange(
        *scaled, lambda tie: swap(lax.optimization_barrier((legendre, *tie))[0], "lev"), plan
    )

    wide = jax.ShapeDtypeStruct((width, width), bf16)
    to_wide, from_wide, rate = call(
        widen_kernel, (wide, wide, jax.ShapeDtypeStruct((width, 1), f32)), "widen", 8
    )(to_modes, from_modes, mode_rates[None, :])
    spec_shape = jax.ShapeDtypeStruct((half, width), bf16)
    spec_mine, spec_other, *parts = call(
        functools.partial(solve_kernel, plan=plan),
        (spec_shape, spec_shape) + pieces,
        "solve",
        20,
        (pltpu.VMEM((2 * half, width), bf16),) * 3,
        [SMEM] + [VMEM] * 7,
    )(slot_wave, keep, got, legendre, table_other, to_wide, from_wide, rate)
    def swap_spectral(tie):
        return swap(lax.optimization_barrier((spec_other, *tie))[0], "lev")

    keep, got, spec_got = exchange(*parts, swap_spectral, plan)
    columns, spectral = call(
        functools.partial(place_kernel, plan=plan),
        (
            jax.ShapeDtypeStruct((rows, waves, side), bf16),
            jax.ShapeDtypeStruct((half, 2 * width), bf16),
        ),
        "place",
        16,
        (
            held,
            wide_rows,
            pltpu.VMEM((rows, waves, side), bf16),
            pltpu.SemaphoreType.DMA((7,)),
        ),
        [SMEM] + [VMEM] * 4,
        HBM,
    )(slot_wave, keep, got, spec_mine, spec_got)
    return (columns[None], spectral[None])


def widen_matrix(square):
    levels = square.shape[0]
    pair_eye = jnp.eye(2, dtype=jnp.float32)
    return (square[:, None, :, None] * pair_eye[None, :, None, :]).reshape(2 * levels, 2 * levels)


def per_device_many(fourier, legendre, quad_weights, slot_wave, to_modes, from_modes, mode_rates):
    parity = lax.axis_index("parity")
    signed_one = (1 - 2 * parity).astype(jnp.float32)
    levels = to_modes.shape[0]
    col_width = 2 * levels
    wave_count = slot_wave.shape[0]
    per_owner = legendre.shape[0]
    degrees = legendre.shape[3]
    top_degree = 2 * degrees - 1
    grid_block = fourier[0]
    scaled = (quad_weights[:, None, None] * grid_block.astype(jnp.float32)).astype(jnp.bfloat16)
    scaled = combine(scaled, partner_2(scaled, "parity", 0), signed_one)
    by_slot = jnp.transpose(jnp.take(scaled, slot_wave, axis=1), (1, 0, 2))
    arrived = lax.all_to_all(
        lax.all_to_all(by_slot, "wave", split_axis=0, concat_axis=1, tiled=True),
        "lev",
        split_axis=1,
        concat_axis=2,
        tiled=True,
    )
    owned_waves = lax.dynamic_slice_in_dim(slot_wave, lax.axis_index("wave") * per_owner, per_owner)
    to_wide = widen_matrix(jnp.transpose(to_modes))
    from_wide = widen_matrix(jnp.transpose(from_modes))
    rates_wide = jnp.repeat(mode_rates, 2)
    half_deg = degrees // lax.axis_size("lev")
    pieces = []
    for owned in range(per_owner):
        deg_block = legendre[owned, 0]
        pieces.append(
            lax.dot_general(
                deg_block,
                arrived[owned],
                (((0,), (0,)), ((), ())),
                preferred_element_type=jnp.float32,
            )
        )
    summed = lax.psum(jnp.concatenate(pieces, axis=1), "lev")
    row_count = summed.shape[0]
    degree_idx = jnp.arange(row_count, dtype=jnp.int32)
    degree = (owned_waves[None, :] + 2 * degree_idx[:, None] + parity).reshape(-1, 1)
    flat = summed.reshape(-1, col_width)
    kept = jnp.where(degree <= top_degree, flat, jnp.zeros_like(flat))
    degree_f = degree.astype(jnp.float32)
    stiffness = degree_f * (degree_f + 1.0) / (top_degree * (top_degree + 1.0))
    mode_part = jnp.dot(
        kept, to_wide, precision=lax.Precision.HIGHEST, preferred_element_type=jnp.float32
    )
    mode_part = mode_part / (1.0 + stiffness * rates_wide[None, :])
    updated = jnp.dot(
        mode_part, from_wide, precision=lax.Precision.HIGHEST, preferred_element_type=jnp.float32
    )
    updated = updated.reshape(row_count, per_owner * col_width).astype(jnp.bfloat16)
    sums = []
    for owned in range(per_owner):
        deg_block = legendre[owned, 0]
        coeffs = updated[:, owned * col_width : (owned + 1) * col_width]
        sums.append(jnp.dot(deg_block, coeffs, preferred_element_type=jnp.float32))
    grid_sums = jnp.stack(sums)
    spectral_mine = lax.dynamic_slice_in_dim(updated, lax.axis_index("lev") * half_deg, half_deg, 0)
    parts = grid_sums.astype(jnp.bfloat16)
    returned = lax.all_to_all(
        lax.all_to_all(parts, "lev", split_axis=2, concat_axis=1, tiled=True),
        "wave",
        split_axis=1,
        concat_axis=0,
        tiled=True,
    )
    returned = combine(returned, partner_2(returned, "parity", 0), signed_one)
    inverse_slot = (
        jnp.zeros((wave_count,), jnp.int32)
        .at[slot_wave]
        .set(jnp.arange(wave_count, dtype=jnp.int32))
    )
    columns = jnp.transpose(jnp.take(returned, inverse_slot, axis=0), (1, 0, 2))
    return (columns[None], spectral_mine[None])


def solution(mesh):
    in_specs = (
        P("parity", "wave", None, "lev"),
        P("wave", "parity", "lev", None),
        P("wave"),
        P(),
        P(),
        P(),
        P(),
    )
    out_specs = (P("parity", "wave", None, "lev"), P("parity", "lev", "wave"))
    few = mesh.shape["wave"] in (8, 16) and mesh.shape["lev"] == mesh.shape["parity"] == 2
    return jax.shard_map(
        per_device if few else per_device_many,
        mesh=mesh,
        in_specs=in_specs,
        out_specs=out_specs,
        check_vma=False,
    )
```
